32 devices in a mesh: dp: 8 (over z, x), tensor: 4 (over y, core).
Axes of the slice: x: 2, y: 2, z: 4, core: 2. Of those that a mesh axis runs over, the one named last changes fastest.
Arguments:
- block_input: bfloat16 [8192, 768], P('dp'), may hold values from -6 to 6
- block_order: int32 [1, 8], replicated, may hold values from 0 to 7, each once within a row
- attn_norm_gain: float32 [768], replicated, may hold values from 0.5 to 1.5
- attn_norm_bias: float32 [768], replicated, may hold values from -1.8 to 1.8
- input_weight: bfloat16 [3, 768, 768], P(None, None, 'tensor'), may hold values from -0.21875 to 0.21875
- query_value_bias: float32 [2, 768], P(None, 'tensor'), may hold values from -3 to 3
- output_weight: bfloat16 [768, 768], P('tensor'), may hold values from -3 to 3
- output_bias: float32 [768], replicated, may hold values from -1.8 to 1.8
- feed_norm_gain: float32 [768], replicated, may hold values from 0.5 to 1.5
- feed_norm_bias: float32 [768], replicated, may hold values from -1.8 to 1.8
- expand_weight: bfloat16 [768, 3072], P(None, 'tensor'), may hold values from -0.21875 to 0.21875
- expand_bias: float32 [3072], P('tensor'), may hold values from -3 to 3
- shrink_weight: bfloat16 [3072, 768], P('tensor'), may hold values from -0.109375 to 0.109375
- shrink_bias: float32 [768], replicated, may hold values from -1.8 to 1.8
- output_grad: bfloat16 [8192, 768], P('dp'), may hold values from -6 to 6
Outputs:
- block_output: bfloat16 [8192, 768], P('dp')
- input_grad: bfloat16 [8192, 768], P('dp')
- attn_norm_gain_grad: float32 [768], replicated
- attn_norm_bias_grad: float32 [768], replicated
- input_weight_grad: float32 [3, 768, 768], P(None, None, 'tensor')
- query_value_bias_grad: float32 [2, 768], P(None, 'tensor')
- output_weight_grad: float32 [768, 768], P('tensor')
- output_bias_grad: float32 [768], replicated
- feed_norm_gain_grad: float32 [768], replicated
- feed_norm_bias_grad: float32 [768], replicated
- expand_weight_grad: float32 [768, 3072], P(None, 'tensor')
- expand_bias_grad: float32 [3072], P('tensor')
- shrink_weight_grad: float32 [3072, 768], P('tensor')
- shrink_bias_grad: float32 [768], replicated
The draws below stay inside these ranges and needn't reach their ends.
Inputs may be any that keep to these rules, and one draw needn't show every extreme that they name: Each row of block_order lists every block number 0 to 7 once.
All inputs are finite; a program needn't handle non-finite values.
Results may differ from the reference program's by a relative error of at most 0.018.
Values may be sent and summed in bfloat16 or wider, within the bound.
A program may use at most 128 MiB of HBM per device.

```python
import jax
import jax.numpy as jnp
from jax import lax

D = 768
HEADS = 12
HEAD_DIM = 64
FF = 3072
GROUP = 8
TOK_DEV = 1024
SEQ = 8192
NSEQ = 1
TOKENS = 8192


def levels(key, extent, split, smallest, largest):
    factor_of = 1.0
    for position, shards_of in split:
        steps = jax.random.uniform(jax.random.fold_in(jax.random.fold_in(key, 6), position), (shards_of,), jnp.float32, smallest / len(split), largest / len(split))
        factor_of = factor_of * jnp.repeat(jnp.exp(steps), extent[position] // shards_of).reshape((-1,) + (1,) * (len(extent) - 1 - position))
    return factor_of


def bell_draw(key, extent, deviation, bound, pieces=(), kind=jnp.bfloat16):
    array = deviation * jax.random.normal(key, extent, jnp.float32)
    if pieces:
        array = array * levels(key, extent, pieces, -0.22, 0.18)
    return jnp.clip(array, -bound, bound).astype(kind)


def setup_inputs(seed: int = 0) -> dict:
    key_of = jax.random.split(jax.random.key(seed), 16)
    block_input = bell_draw(key_of[0], (TOKENS, D), 1.0, 6.0, ((0, 8),))
    block_order = jax.vmap(lambda own: jax.random.permutation(own, GROUP))(jax.random.split(key_of[1], NSEQ)).reshape((NSEQ, GROUP)).astype(jnp.int32)
    attn_norm_gain = jnp.clip(1.0 + 0.1 * jax.random.normal(key_of[2], (D,), jnp.float32), 0.5, 1.5)
    attn_norm_bias = bell_draw(key_of[3], (D,), 0.3, 1.8, (), jnp.float32)
    input_weight = bell_draw(key_of[4], (3, D, D), D ** -0.5, 0.21875, ((2, 4),))
    query_value_bias = bell_draw(key_of[5], (2, D), 0.5, 3.0, ((1, 4),), jnp.float32)
    output_weight = bell_draw(key_of[6], (D, D), 4 ** -0.5, 3.0, ((0, 4),))
    output_bias = bell_draw(key_of[7], (D,), 0.3, 1.8, (), jnp.float32)
    feed_norm_gain = jnp.clip(1.0 + 0.1 * jax.random.normal(key_of[8], (D,), jnp.float32), 0.5, 1.5)
    feed_norm_bias = bell_draw(key_of[9], (D,), 0.3, 1.8, (), jnp.float32)
    expand_weight = bell_draw(key_of[10], (D, FF), D ** -0.5, 0.21875, ((1, 4),))
    expand_bias = bell_draw(key_of[11], (FF,), 0.5, 3.0, ((0, 4),), jnp.float32)
    shrink_weight = bell_draw(key_of[12], (FF, D), FF ** -0.5, 0.109375, ((0, 4),))
    shrink_bias = bell_draw(key_of[13], (D,), 0.3, 1.8, (), jnp.float32)
    output_grad = bell_draw(key_of[14], (TOKENS, D), 1.0, 6.0, ((0, 8),))
    return {"block_input": block_input, "block_order": block_order, "attn_norm_gain": attn_norm_gain, "attn_norm_bias": attn_norm_bias, "input_weight": input_weight, "query_value_bias": query_value_bias, "output_weight": output_weight, "output_bias": output_bias, "feed_norm_gain": feed_norm_gain, "feed_norm_bias": feed_norm_bias, "expand_weight": expand_weight, "expand_bias": expand_bias, "shrink_weight": shrink_weight, "shrink_bias": shrink_bias, "output_grad": output_grad}


@jax.custom_vjp
def low(v):
    return lax.optimization_barrier(v.astype(jnp.bfloat16)).astype(jnp.float32)

@jax.custom_vjp
def low_back(v):
    return v

def low_keep(v):
    return (low(v), None)

def low_pass(kept, grad):
    return (grad,)

def back_keep(v):
    return (v, None)

def back_low(kept, grad):
    return (low(grad),)
low.defvjp(low_keep, low_pass)
low_back.defvjp(back_keep, back_low)
EPSILON = 1e-05
MASKED_SCORE = -1e+30
HIGH = lax.Precision.HIGHEST

def layer_norm(rows, gain, bias_vec):
    center = lax.optimization_barrier(jnp.mean(rows, axis=-1, keepdims=True))
    centred = rows - center
    spread = lax.optimization_barrier(jnp.mean(centred * centred, axis=-1, keepdims=True))
    return centred * lax.rsqrt(spread + EPSILON) * gain + bias_vec

def matmul(left, right):
    return jnp.dot(left, right, precision=HIGH, preferred_element_type=jnp.float32)

def attend_block(query_block, key_heads, value_heads, first_row):
    scores = jnp.einsum('qhd,khd->hqk', query_block, key_heads, precision=HIGH) * HEAD_DIM ** (-0.5)
    scores = low_back(scores)
    query_place = first_row + jnp.arange(query_block.shape[0], dtype=jnp.int32)
    key_place = jnp.arange(key_heads.shape[0], dtype=jnp.int32)
    allowed = key_place[None, None, :] <= query_place[None, :, None]
    masked = jnp.where(allowed, scores, MASKED_SCORE)
    peak = lax.optimization_barrier(jnp.max(masked, axis=-1, keepdims=True))
    expo = jnp.where(allowed, jnp.exp(masked - peak), 0.0)
    probs = expo / lax.optimization_barrier(jnp.sum(expo, axis=-1, keepdims=True))
    return jnp.einsum('hqk,khd->qhd', low(probs), value_heads, precision=HIGH)

def attend_sequence(operands):
    query_heads, key_heads, value_heads = operands
    block_len = min(512, SEQ)
    blocks = SEQ // block_len
    shaped = query_heads.reshape(blocks, block_len, HEADS, HEAD_DIM)
    firsts = jnp.arange(blocks, dtype=jnp.int32) * block_len
    blockwise = jax.checkpoint(attend_block)

    def one_block(item):
        return blockwise(item[0], key_heads, value_heads, item[1])
    result = lax.map(one_block, (shaped, firsts))
    return result.reshape(SEQ, HEADS * HEAD_DIM)

def reference(block_input, block_order, attn_norm_gain, attn_norm_bias, input_weight, query_value_bias, output_weight, output_bias, feed_norm_gain, feed_norm_bias, expand_weight, expand_bias, shrink_weight, shrink_bias, output_grad):
    seq_ids = jnp.arange(NSEQ, dtype=jnp.int32)
    member_ids = jnp.broadcast_to(jnp.arange(GROUP, dtype=jnp.int32)[None, :], (NSEQ, GROUP))
    holder = jnp.zeros((NSEQ, GROUP), jnp.int32).at[seq_ids[:, None], block_order].set(member_ids)
    offsets = jnp.arange(TOK_DEV, dtype=jnp.int32)
    gather_rows = ((seq_ids[:, None, None] * GROUP + holder[:, :, None]) * TOK_DEV + offsets[None, None, :]).reshape(NSEQ * SEQ)
    place_rows = (seq_ids[:, None, None] * SEQ + block_order[:, :, None] * TOK_DEV + offsets[None, None, :]).reshape(TOKENS)

    def forward(inputs, gain_one, bias_one, proj_weight, proj_bias, out_weight, out_bias, gain_two, bias_two, fc_weight, fc_bias, back_weight, back_bias):
        normed_one = low(layer_norm(inputs, gain_one, bias_one))
        queries = low_back(low(matmul(normed_one, proj_weight[0]) + proj_bias[0]))
        keys = low_back(low(matmul(normed_one, proj_weight[1])))
        values = low_back(low(matmul(normed_one, proj_weight[2]) + proj_bias[1]))

        def to_heads(rows):
            return jnp.take(rows, gather_rows, axis=0).reshape(NSEQ, SEQ, HEADS, HEAD_DIM)
        context_seq = lax.map(attend_sequence, (to_heads(queries), to_heads(keys), to_heads(values)))
        context = jnp.take(context_seq.reshape(NSEQ * SEQ, D), place_rows, axis=0)
        context_low = low_back(low(context))
        resid = inputs + low_back(matmul(context_low, out_weight) + out_bias)
        normed_two = low(layer_norm(resid, gain_two, bias_two))
        hidden_pre = low_back(matmul(normed_two, fc_weight) + fc_bias)
        hidden_low = low(jax.nn.gelu(hidden_pre, approximate=True))
        return resid + low_back(matmul(hidden_low, back_weight) + back_bias)
    primals = (block_input.astype(jnp.float32), attn_norm_gain, attn_norm_bias, input_weight.astype(jnp.float32), query_value_bias, output_weight.astype(jnp.float32), output_bias, feed_norm_gain, feed_norm_bias, expand_weight.astype(jnp.float32), expand_bias, shrink_weight.astype(jnp.float32), shrink_bias)
    result, pullback = jax.vjp(forward, *primals)
    grads = pullback(output_grad.astype(jnp.float32))
    return (result.astype(jnp.bfloat16), grads[0].astype(jnp.bfloat16), grads[1], grads[2], grads[3], grads[4], grads[5], grads[6], grads[7], grads[8], grads[9], grads[10], grads[11], grads[12])
```

```python
import functools

import jax
import jax.numpy as jnp
from jax import lax
from jax.experimental import pallas as pl
from jax.experimental.pallas import tpu as pltpu
from jax.sharding import PartitionSpec as P

HEAD_DIM = 64
GROUP = 8


EPSILON = 1e-05
MASKED_SCORE = -1e30
RING = (0, 2, 4, 6, 7, 5, 3, 1)
TILE = 256
VMEM_BYTES = 48 * 1024 * 1024


def ring_shift(value, step):
    pairs = []
    for first in range(0, lax.axis_size("dp"), GROUP):
        for place in range(GROUP):
            pairs.append((first + RING[place], first + RING[(place + step) % GROUP]))
    return lax.ppermute(value, "dp", pairs)


def tdot(left, right, left_dim, right_dim):
    return lax.dot_general(
        left, right, (((left_dim,), (right_dim,)), ((), ())), preferred_element_type=jnp.float32
    )


def forward_kernel(heads, blocks, diagonal, *refs):
    flags, q_ref = refs[:2]
    kv_refs = refs[2 : 2 + 2 * blocks]
    carry_in = refs[2 + 2 * blocks : -3]
    max_ref, sum_ref, acc_ref = refs[-3:]
    tile = q_ref.shape[1]
    if diagonal:
        max_ref[...] = jnp.full(max_ref.shape, MASKED_SCORE, jnp.float32)
        sum_ref[...] = jnp.zeros(sum_ref.shape, jnp.float32)
        acc_ref[...] = jnp.zeros(acc_ref.shape, jnp.float32)
    else:
        max_ref[...] = carry_in[0][...]
        sum_ref[...] = carry_in[1][...]
        acc_ref[...] = carry_in[2][...]
    first_query = pl.program_id(0) * tile

    def block(k_ref, v_ref):
        for head in range(heads):
            rows = slice(head * HEAD_DIM, (head + 1) * HEAD_DIM)
            scores = tdot(k_ref[rows, :], q_ref[rows, :], 0, 0)
            if diagonal:
                key_place = lax.broadcasted_iota(jnp.int32, scores.shape, 0)
                query_place = lax.broadcasted_iota(jnp.int32, scores.shape, 1) + first_query
                scores = jnp.where(key_place <= query_place, scores, MASKED_SCORE)
            old = max_ref[head : head + 1, :]
            new = jnp.maximum(old, jnp.max(scores, axis=0, keepdims=True))
            weights = jnp.exp(scores - new)
            shrink = jnp.exp(old - new)
            max_ref[head : head + 1, :] = new
            sum_ref[head : head + 1, :] = sum_ref[head : head + 1, :] * shrink + jnp.sum(
                weights, axis=0, keepdims=True
            )
            acc_ref[rows, :] = acc_ref[rows, :] * shrink + tdot(
                v_ref[rows, :], weights.astype(jnp.bfloat16), 1, 0
            )

    for index in range(blocks):
        k_ref, v_ref = kv_refs[2 * index : 2 * index + 2]
        if diagonal:
            block(k_ref, v_ref)
        else:
            pl.when(flags[index] > 0)(functools.partial(block, k_ref, v_ref))


def attend_forward(flags, query_t, blocks, carried):
    width, tokens = query_t.shape
    heads = width // HEAD_DIM
    diagonal = carried is None
    in_specs = [
        pl.BlockSpec(memory_space=pltpu.SMEM),
        pl.BlockSpec((width, TILE), lambda i: (0, i)),
    ]
    operands = [flags, query_t]
    for pair in blocks:
        for array, half in pair:
            in_specs.append(pl.BlockSpec((width, tokens), lambda i, half=half: (half, 0)))
            operands.append(array)
    carry_specs = [
        pl.BlockSpec((heads, TILE), lambda i: (0, i)),
        pl.BlockSpec((heads, TILE), lambda i: (0, i)),
        pl.BlockSpec((width, TILE), lambda i: (0, i)),
    ]
    if not diagonal:
        in_specs.extend(carry_specs)
        operands.extend(carried)
    pairs = len(blocks) * heads * tokens * tokens
    return pl.pallas_call(
        functools.partial(forward_kernel, heads, len(blocks), diagonal),
        grid=(tokens // TILE,),
        in_specs=in_specs,
        out_specs=carry_specs,
        out_shape=[
            jax.ShapeDtypeStruct((heads, tokens), jnp.float32),
            jax.ShapeDtypeStruct((heads, tokens), jnp.float32),
            jax.ShapeDtypeStruct((width, tokens), jnp.float32),
        ],
        compiler_params=pltpu.CompilerParams(vmem_limit_bytes=VMEM_BYTES),
        cost_estimate=pl.CostEstimate(
            flops=16 * pairs * HEAD_DIM, bytes_accessed=4 * width * tokens * 4, transcendentals=pairs
        ),
    )(*operands)


def backward_kernel(heads, blocks, diagonal, *refs):
    flags, q_ref, grad_ref, log_ref, delta_ref = refs[:5]
    kv_refs = refs[5 : 5 + 2 * blocks]
    query_in = refs[5 + 2 * blocks]
    query_out = refs[6 + 2 * blocks]
    kv_out = refs[7 + 2 * blocks :]
    step = pl.program_id(0)
    tile = kv_refs[0].shape[1]
    width = heads * HEAD_DIM

    @pl.when(step == 0)
    def start():
        query_out[...] = query_in[...]

    def block(k_ref, v_ref, out_ref):
        for head in range(heads):
            rows = slice(head * HEAD_DIM, (head + 1) * HEAD_DIM)
            query = q_ref[rows, :]
            grad = grad_ref[rows, :]
            key = k_ref[rows, :]
            scores = tdot(key, query, 0, 0)
            probs = jnp.exp(scores - log_ref[head : head + 1, :])
            if diagonal:
                key_place = lax.broadcasted_iota(jnp.int32, scores.shape, 0) + step * tile
                query_place = lax.broadcasted_iota(jnp.int32, scores.shape, 1)
                probs = jnp.where(key_place <= query_place, probs, 0.0)
            prob_grad = tdot(v_ref[rows, :], grad, 0, 0)
            score_grad = (probs * (prob_grad - delta_ref[head : head + 1, :])).astype(jnp.bfloat16)
            out_ref[:, rows] = tdot(score_grad, query, 1, 1)
            out_ref[:, width + head * HEAD_DIM : width + (head + 1) * HEAD_DIM] = tdot(
                probs.astype(jnp.bfloat16), grad, 1, 1
            )
            query_out[rows, :] += tdot(key, score_grad, 1, 0)

    for index in range(blocks):
        k_ref, v_ref = kv_refs[2 * index : 2 * index + 2]
        out_ref = kv_out[index]
        if diagonal:
            block(k_ref, v_ref, out_ref)
        else:
            pl.when(flags[index] > 0)(functools.partial(block, k_ref, v_ref, out_ref))

            @pl.when(flags[index] <= 0)
            def empty(out_ref=out_ref):
                out_ref[...] = jnp.zeros(out_ref.shape, jnp.float32)


def attend_backward(flags, query_t, grad_t, log_total, delta, blocks, query_sum, diagonal):
    width, tokens = query_t.shape
    heads = width // HEAD_DIM
    whole = lambda rows: pl.BlockSpec((rows, tokens), lambda i: (0, 0))
    in_specs = [
        pl.BlockSpec(memory_space=pltpu.SMEM),
        whole(width),
        whole(width),
        whole(heads),
        whole(heads),
    ]
    operands = [flags, query_t, grad_t, log_total, delta]
    for pair in blocks:
        for array, half in pair:
            in_specs.append(pl.BlockSpec((width, TILE), lambda i, half=half: (half, i)))
            operands.append(array)
    in_specs.append(whole(width))
    operands.append(query_sum)
    pairs = len(blocks) * heads * tokens * tokens
    return pl.pallas_call(
        functools.partial(backward_kernel, heads, len(blocks), diagonal),
        grid=(tokens // TILE,),
        in_specs=in_specs,
        out_specs=[whole(width)]
        + [pl.BlockSpec((TILE, 2 * width), lambda i: (i, 0)) for unused in blocks],
        out_shape=[jax.ShapeDtypeStruct((width, tokens), jnp.float32)]
        + [jax.ShapeDtypeStruct((tokens, 2 * width), jnp.float32) for unused in blocks],
        compiler_params=pltpu.CompilerParams(vmem_limit_bytes=VMEM_BYTES),
        cost_estimate=pl.CostEstimate(
            flops=40 * pairs * HEAD_DIM, bytes_accessed=6 * width * tokens * 4, transcendentals=pairs
        ),
    )(*operands)


def layer_norm(rows, gain, bias_vec):
    center = jnp.mean(rows, axis=-1, keepdims=True)
    centred = rows - center
    spread = jnp.mean(centred * centred, axis=-1, keepdims=True)
    return centred * lax.rsqrt(spread + EPSILON) * gain + bias_vec


def gelu_tanh(values):
    return jax.nn.gelu(values, approximate=True)


def sum_tokens(value):
    return lax.psum(value, "dp")


def sum_tensor(value):
    return lax.psum(value.astype(jnp.bfloat16), "tensor").astype(jnp.float32)


def local(
    block_input,
    block_order,
    attn_norm_gain,
    attn_norm_bias,
    input_weight,
    query_value_bias,
    output_weight,
    output_bias,
    feed_norm_gain,
    feed_norm_bias,
    expand_weight,
    expand_bias,
    shrink_weight,
    shrink_bias,
    output_grad,
):
    dp_index = lax.axis_index("dp")
    tok_rows = block_input.shape[0]
    local_width = input_weight.shape[2]
    local_heads = local_width // HEAD_DIM
    scale = HEAD_DIM ** (-0.5)
    order_row = lax.dynamic_index_in_dim(block_order, dp_index // GROUP, 0, keepdims=False)
    ring_order = order_row[jnp.array(RING)]
    ring_place = jnp.argmax(jnp.array(RING) == dp_index % GROUP).astype(jnp.int32)
    own_block = ring_order[ring_place]

    def flags_of(*offsets):
        return jnp.stack(
            [
                (ring_order[(ring_place + offset) % GROUP] < own_block).astype(jnp.int32)
                for offset in offsets
            ]
        )

    inputs32 = block_input.astype(jnp.float32)
    normed_one = layer_norm(inputs32, attn_norm_gain, attn_norm_bias).astype(jnp.bfloat16)
    kv_weight = jnp.concatenate([input_weight[1], input_weight[2]], axis=1)
    kv_bias = jnp.concatenate([jnp.zeros((local_width,), jnp.float32), query_value_bias[1]])
    kv_t = (
        jnp.einsum("td,df->ft", normed_one, kv_weight, preferred_element_type=jnp.float32)
        + kv_bias[:, None]
    ).astype(jnp.bfloat16)
    ups = [kv_t]
    downs = [kv_t]
    ups.append(ring_shift(ups[0], 1))
    downs.append(ring_shift(downs[0], -1))
    query_t = (
        jnp.einsum("td,df->ft", normed_one, input_weight[0], preferred_element_type=jnp.float32)
        + query_value_bias[0][:, None]
    ).astype(jnp.bfloat16)
    query_t = query_t * jnp.bfloat16(scale)
    for hop in (2, 3):
        ups.append(ring_shift(ups[-1], 1))
        downs.append(ring_shift(downs[-1], -1))
    far_keys = ring_shift(ups[-1][:local_width], 1)
    far_values = ring_shift(downs[-1][local_width:], -1)

    def whole_pair(array):
        return ((array, 0), (array, 1))

    own_pair = [whole_pair(kv_t)]
    hop_pairs = [None] + [[whole_pair(ups[hop]), whole_pair(downs[hop])] for hop in (1, 2, 3)]
    far_pair = [((far_keys, 0), (far_values, 0))]
    hop_flags = [None] + [flags_of(-hop, hop) for hop in (1, 2, 3)]
    far_flags = flags_of(4)

    carried = attend_forward(far_flags, query_t, own_pair, None)
    for hop in (1, 2, 3):
        carried = attend_forward(hop_flags[hop], query_t, hop_pairs[hop], carried)
    run_max, run_sum, acc = attend_forward(far_flags, query_t, far_pair, carried)
    log_total = run_max + jnp.log(run_sum)
    context_t = (acc.reshape(local_heads, HEAD_DIM, tok_rows) / run_sum[:, None, :]).reshape(
        local_width, tok_rows
    )
    context_low_t = context_t.astype(jnp.bfloat16)
    attn_part = jnp.einsum(
        "ct,cd->td", context_low_t, output_weight, preferred_element_type=jnp.float32
    )
    resid = inputs32 + sum_tensor(attn_part) + output_bias
    normed_two = layer_norm(resid, feed_norm_gain, feed_norm_bias).astype(jnp.bfloat16)
    hidden_pre = (
        jnp.dot(normed_two, expand_weight, preferred_element_type=jnp.float32) + expand_bias
    )
    hidden_grad = jnp.einsum(
        "td,fd->tf", output_grad, shrink_weight, preferred_element_type=jnp.float32
    )
    hidden, gelu_pull = jax.vjp(gelu_tanh, hidden_pre)
    hidden_low = hidden.astype(jnp.bfloat16)
    pre_grad = gelu_pull(hidden_grad)[0].astype(jnp.bfloat16)
    two_part = jnp.einsum("tf,df->td", pre_grad, expand_weight, preferred_element_type=jnp.float32)
    normed_two_grad = sum_tensor(two_part)
    feed_part = jnp.dot(hidden_low, shrink_weight, preferred_element_type=jnp.float32)
    block_output = (resid + sum_tensor(feed_part) + shrink_bias).astype(jnp.bfloat16)
    grad_out32 = output_grad.astype(jnp.float32)
    shrink_weight_grad = jnp.einsum(
        "tf,td->fd", hidden_low, output_grad, preferred_element_type=jnp.float32
    )
    expand_weight_grad = jnp.einsum(
        "td,tf->df", normed_two, pre_grad, preferred_element_type=jnp.float32
    )
    feed_grads = sum_tokens(
        jnp.concatenate([shrink_weight_grad, expand_weight_grad], axis=0).astype(jnp.bfloat16)
    ).astype(jnp.float32)
    shrink_bias_grad = jnp.sum(grad_out32, axis=0)
    expand_bias_grad = jnp.sum(pre_grad.astype(jnp.float32), axis=0)
    unused_norm, norm_two_pull = jax.vjp(layer_norm, resid, feed_norm_gain, feed_norm_bias)
    resid_part, feed_norm_gain_grad, feed_norm_bias_grad = norm_two_pull(normed_two_grad)
    resid_grad = grad_out32 + resid_part
    branch_grad = resid_grad.astype(jnp.bfloat16)
    output_bias_grad = jnp.sum(branch_grad.astype(jnp.float32), axis=0)
    grad_t = jnp.einsum(
        "td,cd->ct", branch_grad, output_weight, preferred_element_type=jnp.float32
    ).astype(jnp.bfloat16)
    delta = jnp.sum(
        (grad_t.astype(jnp.float32) * context_t).reshape(local_heads, HEAD_DIM, tok_rows), axis=1
    )

    def back(flags, blocks, query_sum, diagonal):
        return attend_backward(
            flags, query_t, grad_t, log_total, delta, blocks, query_sum, diagonal
        )

    query_sum = jnp.zeros((local_width, tok_rows), jnp.float32)
    query_sum, far_term = back(far_flags, far_pair, query_sum, False)
    far_low = far_term.astype(jnp.bfloat16)
    moving_up = ring_shift(far_low[:, :local_width], 1)
    moving_down = ring_shift(far_low[:, local_width:], -1)
    for hop in (3, 2, 1):
        query_sum, down_term, up_term = back(hop_flags[hop], hop_pairs[hop], query_sum, False)
        if hop == 3:
            up_sum = jnp.concatenate(
                [
                    up_term[:, :local_width] + moving_up.astype(jnp.float32),
                    up_term[:, local_width:],
                ],
                axis=1,
            )
            down_sum = jnp.concatenate(
                [
                    down_term[:, :local_width],
                    down_term[:, local_width:] + moving_down.astype(jnp.float32),
                ],
                axis=1,
            )
        else:
            up_sum = up_term + moving_up.astype(jnp.float32)
            down_sum = down_term + moving_down.astype(jnp.float32)
        moving_up = ring_shift(up_sum.astype(jnp.bfloat16), 1)
        moving_down = ring_shift(down_sum.astype(jnp.bfloat16), -1)
    query_sum, own_term = back(far_flags, own_pair, query_sum, True)
    kv_low = (
        own_term + moving_up.astype(jnp.float32) + moving_down.astype(jnp.float32)
    ).astype(jnp.bfloat16)
    query_low_t = (query_sum * scale).astype(jnp.bfloat16)
    one_part = jnp.einsum(
        "ft,df->td", query_low_t, input_weight[0], preferred_element_type=jnp.float32
    ) + jnp.einsum("tf,df->td", kv_low, kv_weight, preferred_element_type=jnp.float32)
    normed_one_grad = sum_tensor(one_part)
    output_weight_grad_t = jnp.einsum(
        "ct,td->dc", context_low_t, branch_grad, preferred_element_type=jnp.float32
    )
    query_weight_grad = jnp.einsum(
        "td,ft->df", normed_one, query_low_t, preferred_element_type=jnp.float32
    )
    kv_weight_grad = jnp.einsum(
        "td,tf->df", normed_one, kv_low, preferred_element_type=jnp.float32
    )
    attn_grads = sum_tokens(
        jnp.concatenate(
            [query_weight_grad, kv_weight_grad, output_weight_grad_t], axis=1
        ).astype(jnp.bfloat16)
    ).astype(jnp.float32)
    input_weight_grad = jnp.stack(
        [attn_grads[:, j * local_width : (j + 1) * local_width] for j in range(3)]
    )
    output_weight_grad = jnp.transpose(attn_grads[:, 3 * local_width :])
    query_bias_grad = jnp.sum(query_low_t.astype(jnp.float32), axis=1)
    value_bias_grad = jnp.sum(kv_low[:, local_width:].astype(jnp.float32), axis=0)
    unused_first, norm_one_pull = jax.vjp(layer_norm, inputs32, attn_norm_gain, attn_norm_bias)
    input_part, attn_norm_gain_grad, attn_norm_bias_grad = norm_one_pull(normed_one_grad)
    input_grad = (resid_grad + input_part).astype(jnp.bfloat16)
    vectors = [
        attn_norm_gain_grad,
        attn_norm_bias_grad,
        output_bias_grad,
        feed_norm_gain_grad,
        feed_norm_bias_grad,
        expand_bias_grad,
        shrink_bias_grad,
        query_bias_grad,
        value_bias_grad,
    ]
    joined = sum_tokens(jnp.concatenate(vectors))
    summed = []
    first = 0
    for vector in vectors:
        summed.append(joined[first : first + vector.shape[0]])
        first += vector.shape[0]
    ff_rows = shrink_weight.shape[0]
    return (
        block_output,
        input_grad,
        summed[0],
        summed[1],
        input_weight_grad,
        jnp.stack([summed[7], summed[8]]),
        output_weight_grad,
        summed[2],
        summed[3],
        summed[4],
        feed_grads[ff_rows:],
        summed[5],
        feed_grads[:ff_rows],
        summed[6],
    )


def solution(mesh):
    placed = (
        P("dp", None),
        P(),
        P(),
        P(),
        P(None, None, "tensor"),
        P(None, "tensor"),
        P("tensor", None),
        P(),
        P(),
        P(),
        P(None, "tensor"),
        P("tensor"),
        P("tensor", None),
        P(),
        P("dp", None),
    )
    return jax.shard_map(
        local,
        mesh=mesh,
        in_specs=placed,
        out_specs=(
            P("dp", None),
            P("dp", None),
            P(),
            P(),
            P(None, None, "tensor"),
            P(None, "tensor"),
            P("tensor", None),
            P(),
            P(),
            P(),
            P(None, "tensor"),
            P("tensor"),
            P("tensor", None),
            P(),
        ),
        check_vma=False,
    )
```

```python
import functools

import jax
import jax.numpy as jnp
from jax import lax
from jax.experimental import pallas as pl
from jax.experimental.pallas import tpu as pltpu
from jax.sharding import PartitionSpec as P

HEAD_DIM = 64
GROUP = 8


EPSILON = 1e-05
MASKED_SCORE = -1e30
RING = (0, 2, 4, 6, 7, 5, 3, 1)
TILE = 256
VMEM_BYTES = 48 * 1024 * 1024


def ring_shift(value, step):
    pairs = []
    for first in range(0, lax.axis_size("dp"), GROUP):
        for place in range(GROUP):
            pairs.append((first + RING[place], first + RING[(place + step) % GROUP]))
    return lax.ppermute(value, "dp", pairs)


def tdot(left, right, left_dim, right_dim):
    return lax.dot_general(
        left, right, (((left_dim,), (right_dim,)), ((), ())), preferred_element_type=jnp.float32
    )


def forward_kernel(heads, blocks, diagonal, *refs):
    flags, q_ref = refs[:2]
    kv_refs = refs[2 : 2 + 2 * blocks]
    carry_in = refs[2 + 2 * blocks : -3]
    max_ref, sum_ref, acc_ref = refs[-3:]
    tile = q_ref.shape[1]
    if diagonal:
        max_ref[...] = jnp.full(max_ref.shape, MASKED_SCORE, jnp.float32)
        sum_ref[...] = jnp.zeros(sum_ref.shape, jnp.float32)
        acc_ref[...] = jnp.zeros(acc_ref.shape, jnp.float32)
    else:
        max_ref[...] = carry_in[0][...]
        sum_ref[...] = carry_in[1][...]
        acc_ref[...] = carry_in[2][...]
    first_query = pl.program_id(0) * tile

    def block(k_ref, v_ref):
        spans = [slice(head * HEAD_DIM, (head + 1) * HEAD_DIM) for head in range(heads)]
        scores = [tdot(k_ref[rows, :], q_ref[rows, :], 0, 0) for rows in spans]
        if diagonal:
            key_place = lax.broadcasted_iota(jnp.int32, scores[0].shape, 0)
            query_place = lax.broadcasted_iota(jnp.int32, scores[0].shape, 1) + first_query
            allowed = key_place <= query_place
            scores = [jnp.where(allowed, part, MASKED_SCORE) for part in scores]
        olds = [max_ref[head : head + 1, :] for head in range(heads)]
        sums = [sum_ref[head : head + 1, :] for head in range(heads)]
        accs = [acc_ref[rows, :] for rows in spans]
        news = [
            jnp.maximum(old, jnp.max(part, axis=0, keepdims=True))
            for old, part in zip(olds, scores)
        ]
        weights = [jnp.exp(part - new) for part, new in zip(scores, news)]
        shrinks = [jnp.exp(old - new) for old, new in zip(olds, news)]
        sums = [
            total * shrink + jnp.sum(part, axis=0, keepdims=True)
            for total, shrink, part in zip(sums, shrinks, weights)
        ]
        accs = [
            acc * shrink + tdot(v_ref[rows, :], part.astype(jnp.bfloat16), 1, 0)
            for acc, shrink, rows, part in zip(accs, shrinks, spans, weights)
        ]
        for head, rows in enumerate(spans):
            max_ref[head : head + 1, :] = news[head]
            sum_ref[head : head + 1, :] = sums[head]
            acc_ref[rows, :] = accs[head]

    for index in range(blocks):
        k_ref, v_ref = kv_refs[2 * index : 2 * index + 2]
        if diagonal:
            block(k_ref, v_ref)
        else:
            pl.when(flags[index] > 0)(functools.partial(block, k_ref, v_ref))


def attend_forward(flags, query_t, blocks, carried):
    width, tokens = query_t.shape
    heads = width // HEAD_DIM
    diagonal = carried is None
    in_specs = [
        pl.BlockSpec(memory_space=pltpu.SMEM),
        pl.BlockSpec((width, TILE), lambda i: (0, i)),
    ]
    operands = [flags, query_t]
    for pair in blocks:
        for array, half in pair:
            in_specs.append(pl.BlockSpec((width, tokens), lambda i, half=half: (half, 0)))
            operands.append(array)
    carry_specs = [
        pl.BlockSpec((heads, TILE), lambda i: (0, i)),
        pl.BlockSpec((heads, TILE), lambda i: (0, i)),
        pl.BlockSpec((width, TILE), lambda i: (0, i)),
    ]
    if not diagonal:
        in_specs.extend(carry_specs)
        operands.extend(carried)
    pairs = len(blocks) * heads * tokens * tokens
    return pl.pallas_call(
        functools.partial(forward_kernel, heads, len(blocks), diagonal),
        grid=(tokens // TILE,),
        in_specs=in_specs,
        out_specs=carry_specs,
        out_shape=[
            jax.ShapeDtypeStruct((heads, tokens), jnp.float32),
            jax.ShapeDtypeStruct((heads, tokens), jnp.float32),
            jax.ShapeDtypeStruct((width, tokens), jnp.float32),
        ],
        compiler_params=pltpu.CompilerParams(vmem_limit_bytes=VMEM_BYTES),
        cost_estimate=pl.CostEstimate(
            flops=16 * pairs * HEAD_DIM, bytes_accessed=4 * width * tokens * 4, transcendentals=pairs
        ),
    )(*operands)


def backward_kernel(heads, blocks, diagonal, *refs):
    flags, q_ref, grad_ref, log_ref, delta_ref = refs[:5]
    kv_refs = refs[5 : 5 + 2 * blocks]
    query_in = refs[5 + 2 * blocks]
    query_out = refs[6 + 2 * blocks]
    kv_out = refs[7 + 2 * blocks :]
    step = pl.program_id(0)
    tile = kv_refs[0].shape[1]
    width = heads * HEAD_DIM

    @pl.when(step == 0)
    def start():
        query_out[...] = query_in[...]

    def block(k_ref, v_ref, out_ref):
        for head in range(heads):
            rows = slice(head * HEAD_DIM, (head + 1) * HEAD_DIM)
            query = q_ref[rows, :]
            grad = grad_ref[rows, :]
            key = k_ref[rows, :]
            scores = tdot(key, query, 0, 0)
            probs = jnp.exp(scores - log_ref[head : head + 1, :])
            if diagonal:
                key_place = lax.broadcasted_iota(jnp.int32, scores.shape, 0) + step * tile
                query_place = lax.broadcasted_iota(jnp.int32, scores.shape, 1)
                probs = jnp.where(key_place <= query_place, probs, 0.0)
            prob_grad = tdot(v_ref[rows, :], grad, 0, 0)
            score_grad = (probs * (prob_grad - delta_ref[head : head + 1, :])).astype(jnp.bfloat16)
            out_ref[:, rows] = tdot(score_grad, query, 1, 1)
            out_ref[:, width + head * HEAD_DIM : width + (head + 1) * HEAD_DIM] = tdot(
                probs.astype(jnp.bfloat16), grad, 1, 1
            )
            query_out[rows, :] += tdot(key, score_grad, 1, 0)

    for index in range(blocks):
        k_ref, v_ref = kv_refs[2 * index : 2 * index + 2]
        out_ref = kv_out[index]
        if diagonal:
            block(k_ref, v_ref, out_ref)
        else:
            pl.when(flags[index] > 0)(functools.partial(block, k_ref, v_ref, out_ref))

            @pl.when(flags[index] <= 0)
            def empty(out_ref=out_ref):
                out_ref[...] = jnp.zeros(out_ref.shape, jnp.float32)


def attend_backward(flags, query_t, grad_t, log_total, delta, blocks, query_sum, diagonal):
    width, tokens = query_t.shape
    heads = width // HEAD_DIM
    whole = lambda rows: pl.BlockSpec((rows, tokens), lambda i: (0, 0))
    in_specs = [
        pl.BlockSpec(memory_space=pltpu.SMEM),
        whole(width),
        whole(width),
        whole(heads),
        whole(heads),
    ]
    operands = [flags, query_t, grad_t, log_total, delta]
    for pair in blocks:
        for array, half in pair:
            in_specs.append(pl.BlockSpec((width, TILE), lambda i, half=half: (half, i)))
            operands.append(array)
    in_specs.append(whole(width))
    operands.append(query_sum)
    pairs = len(blocks) * heads * tokens * tokens
    return pl.pallas_call(
        functools.partial(backward_kernel, heads, len(blocks), diagonal),
        grid=(tokens // TILE,),
        in_specs=in_specs,
        out_specs=[whole(width)]
        + [pl.BlockSpec((TILE, 2 * width), lambda i: (i, 0)) for unused in blocks],
        out_shape=[jax.ShapeDtypeStruct((width, tokens), jnp.float32)]
        + [jax.ShapeDtypeStruct((tokens, 2 * width), jnp.float32) for unused in blocks],
        compiler_params=pltpu.CompilerParams(vmem_limit_bytes=VMEM_BYTES),
        cost_estimate=pl.CostEstimate(
            flops=40 * pairs * HEAD_DIM, bytes_accessed=6 * width * tokens * 4, transcendentals=pairs
        ),
    )(*operands)


def layer_norm(rows, gain, bias_vec):
    center = jnp.mean(rows, axis=-1, keepdims=True)
    centred = rows - center
    spread = jnp.mean(centred * centred, axis=-1, keepdims=True)
    return centred * lax.rsqrt(spread + EPSILON) * gain + bias_vec


def gelu_tanh(values):
    return jax.nn.gelu(values, approximate=True)


def sum_tokens(value):
    return lax.psum(value, "dp")


def partner(value, axis, mask):
    pairs = [(source, source ^ mask) for source in range(lax.axis_size(axis))]
    return lax.ppermute(value, axis, pairs)


def sum_tokens_small(value):
    mask = 1
    while mask < lax.axis_size("dp"):
        value = value + partner(value, "dp", mask)
        mask *= 2
    return value


def rounded(value):
    return lax.optimization_barrier(value.astype(jnp.bfloat16))


def sum_tensor(value):
    value = rounded(value)
    core = lax.axis_index("tensor") % 2
    half = value.shape[0] // 2
    kept = lax.dynamic_slice_in_dim(value, core * half, half, 0)
    sent = lax.dynamic_slice_in_dim(value, (1 - core) * half, half, 0)
    total = kept.astype(jnp.float32) + partner(sent, "tensor", 1).astype(jnp.float32)
    mask = 2
    while mask < lax.axis_size("tensor"):
        low = rounded(total)
        total = low.astype(jnp.float32) + partner(low, "tensor", mask).astype(jnp.float32)
        mask *= 2
    low = rounded(total)
    other = partner(low, "tensor", 1)
    lower = jnp.where(core == 0, low, other)
    upper = jnp.where(core == 0, other, low)
    return jnp.concatenate([lower, upper], axis=0).astype(jnp.float32)


def local(
    block_input,
    block_order,
    attn_norm_gain,
    attn_norm_bias,
    input_weight,
    query_value_bias,
    output_weight,
    output_bias,
    feed_norm_gain,
    feed_norm_bias,
    expand_weight,
    expand_bias,
    shrink_weight,
    shrink_bias,
    output_grad,
):
    dp_index = lax.axis_index("dp")
    tok_rows = block_input.shape[0]
    local_width = input_weight.shape[2]
    local_heads = local_width // HEAD_DIM
    scale = HEAD_DIM ** (-0.5)
    order_row = lax.dynamic_index_in_dim(block_order, dp_index // GROUP, 0, keepdims=False)
    ring_order = order_row[jnp.array(RING)]
    ring_place = jnp.argmax(jnp.array(RING) == dp_index % GROUP).astype(jnp.int32)
    own_block = ring_order[ring_place]

    def flags_of(*offsets):
        return jnp.stack(
            [
                (ring_order[(ring_place + offset) % GROUP] < own_block).astype(jnp.int32)
                for offset in offsets
            ]
        )

    inputs32 = block_input.astype(jnp.float32)
    normed_one = layer_norm(inputs32, attn_norm_gain, attn_norm_bias).astype(jnp.bfloat16)
    kv_weight = jnp.concatenate([input_weight[1], input_weight[2]], axis=1)
    kv_bias = jnp.concatenate([jnp.zeros((local_width,), jnp.float32), query_value_bias[1]])
    kv_t = (
        jnp.einsum("td,df->ft", normed_one, kv_weight, preferred_element_type=jnp.float32)
        + kv_bias[:, None]
    ).astype(jnp.bfloat16)
    ups = [kv_t]
    downs = [kv_t]
    ups.append(ring_shift(ups[0], 1))
    downs.append(ring_shift(downs[0], -1))
    query_t = (
        jnp.einsum("td,df->ft", normed_one, input_weight[0], preferred_element_type=jnp.float32)
        + query_value_bias[0][:, None]
    ).astype(jnp.bfloat16)
    query_t = query_t * jnp.bfloat16(scale)
    def whole_pair(array):
        return ((array, 0), (array, 1))

    own_pair = [whole_pair(kv_t)]
    hop_pairs = [None]
    hop_flags = [None] + [flags_of(-hop, hop) for hop in (1, 2, 3)]
    far_flags = flags_of(4)
    carried = attend_forward(far_flags, query_t, own_pair, None)
    for hop in (1, 2, 3):
        ups[hop], downs[hop], carried = lax.optimization_barrier((ups[hop], downs[hop], carried))
        hop_pairs.append([whole_pair(ups[hop]), whole_pair(downs[hop])])
        if hop < 3:
            ups.append(ring_shift(ups[hop], 1))
            downs.append(ring_shift(downs[hop], -1))
        else:
            far_keys = ring_shift(ups[hop][:local_width], 1)
            far_values = ring_shift(downs[hop][local_width:], -1)
            far_pair = [((far_keys, 0), (far_values, 0))]
        carried = attend_forward(hop_flags[hop], query_t, hop_pairs[hop], carried)
    run_max, run_sum, acc = attend_forward(far_flags, query_t, far_pair, carried)
    log_total = run_max + jnp.log(run_sum)
    context_t = (acc.reshape(local_heads, HEAD_DIM, tok_rows) / run_sum[:, None, :]).reshape(
        local_width, tok_rows
    )
    context_low_t = context_t.astype(jnp.bfloat16)
    attn_part = jnp.einsum(
        "ct,cd->td", context_low_t, output_weight, preferred_element_type=jnp.float32
    )
    resid = inputs32 + sum_tensor(attn_part) + output_bias
    normed_two = layer_norm(resid, feed_norm_gain, feed_norm_bias).astype(jnp.bfloat16)
    hidden_pre = (
        jnp.dot(normed_two, expand_weight, preferred_element_type=jnp.float32) + expand_bias
    )
    hidden_grad = jnp.einsum(
        "td,fd->tf", output_grad, shrink_weight, preferred_element_type=jnp.float32
    )
    hidden, gelu_pull = jax.vjp(gelu_tanh, hidden_pre)
    hidden_low = hidden.astype(jnp.bfloat16)
    pre_grad = gelu_pull(hidden_grad)[0].astype(jnp.bfloat16)
    two_part = jnp.einsum("tf,df->td", pre_grad, expand_weight, preferred_element_type=jnp.float32)
    normed_two_grad = sum_tensor(two_part)
    feed_part = jnp.dot(
        hidden_low, shrink_weight, preferred_element_type=jnp.float32
    ).astype(jnp.bfloat16)
    grad_out32 = output_grad.astype(jnp.float32)
    shrink_weight_grad = jnp.einsum(
        "tf,td->fd", hidden_low, output_grad, preferred_element_type=jnp.float32
    )
    expand_weight_grad = jnp.einsum(
        "td,tf->df", normed_two, pre_grad, preferred_element_type=jnp.float32
    )
    feed_low = sum_tokens(
        jnp.concatenate([shrink_weight_grad, expand_weight_grad], axis=0).astype(jnp.bfloat16)
    )
    shrink_bias_grad = jnp.sum(grad_out32, axis=0)
    expand_bias_grad = jnp.sum(pre_grad.astype(jnp.float32), axis=0)
    unused_norm, norm_two_pull = jax.vjp(layer_norm, resid, feed_norm_gain, feed_norm_bias)
    resid_part, feed_norm_gain_grad, feed_norm_bias_grad = norm_two_pull(normed_two_grad)
    resid_grad = grad_out32 + resid_part
    branch_grad = resid_grad.astype(jnp.bfloat16)
    output_bias_grad = jnp.sum(branch_grad.astype(jnp.float32), axis=0)
    grad_t = jnp.einsum(
        "td,cd->ct", branch_grad, output_weight, preferred_element_type=jnp.float32
    ).astype(jnp.bfloat16)
    delta = jnp.sum(
        (grad_t.astype(jnp.float32) * context_t).reshape(local_heads, HEAD_DIM, tok_rows), axis=1
    )

    def back(flags, blocks, query_sum, diagonal):
        return attend_backward(
            flags, query_t, grad_t, log_total, delta, blocks, query_sum, diagonal
        )

    query_sum = jnp.zeros((local_width, tok_rows), jnp.float32)
    query_sum, far_term = back(far_flags, far_pair, query_sum, False)
    query_sum, feed_part = lax.optimization_barrier((query_sum, feed_part))
    block_output = (resid + sum_tensor(feed_part) + shrink_bias).astype(jnp.bfloat16)
    far_low = far_term.astype(jnp.bfloat16)
    moving_up = ring_shift(far_low[:, :local_width], 1)
    moving_down = ring_shift(far_low[:, local_width:], -1)
    for hop in (3, 2, 1):
        if hop == 1:
            query_sum, feed_low, block_output = lax.optimization_barrier(
                (query_sum, feed_low, block_output)
            )
        query_sum, down_term, up_term = back(hop_flags[hop], hop_pairs[hop], query_sum, False)
        if hop == 3:
            up_sum = jnp.concatenate(
                [
                    up_term[:, :local_width] + moving_up.astype(jnp.float32),
                    up_term[:, local_width:],
                ],
                axis=1,
            )
            down_sum = jnp.concatenate(
                [
                    down_term[:, :local_width],
                    down_term[:, local_width:] + moving_down.astype(jnp.float32),
                ],
                axis=1,
            )
        else:
            up_sum = up_term + moving_up.astype(jnp.float32)
            down_sum = down_term + moving_down.astype(jnp.float32)
        moving_up = ring_shift(up_sum.astype(jnp.bfloat16), 1)
        moving_down = ring_shift(down_sum.astype(jnp.bfloat16), -1)
    query_sum, own_term = back(far_flags, own_pair, query_sum, True)
    kv_low = (
        own_term + moving_up.astype(jnp.float32) + moving_down.astype(jnp.float32)
    ).astype(jnp.bfloat16)
    query_low_t = (query_sum * scale).astype(jnp.bfloat16)
    one_part = jnp.einsum(
        "ft,df->td", query_low_t, input_weight[0], preferred_element_type=jnp.float32
    ) + jnp.einsum("tf,df->td", kv_low, kv_weight, preferred_element_type=jnp.float32)
    normed_one_grad = sum_tensor(one_part)
    output_weight_grad_t = jnp.einsum(
        "ct,td->dc", context_low_t, branch_grad, preferred_element_type=jnp.float32
    )
    query_weight_grad = jnp.einsum(
        "td,ft->df", normed_one, query_low_t, preferred_element_type=jnp.float32
    )
    kv_weight_grad = jnp.einsum(
        "td,tf->df", normed_one, kv_low, preferred_element_type=jnp.float32
    )
    attn_low = jnp.concatenate(
        [query_weight_grad, kv_weight_grad, output_weight_grad_t], axis=1
    ).astype(jnp.bfloat16)
    attn_low, feed_low = lax.optimization_barrier((attn_low, feed_low))
    attn_grads = sum_tokens(attn_low).astype(jnp.float32)
    feed_grads = feed_low.astype(jnp.float32)
    input_weight_grad = jnp.stack(
        [attn_grads[:, j * local_width : (j + 1) * local_width] for j in range(3)]
    )
    output_weight_grad = jnp.transpose(attn_grads[:, 3 * local_width :])
    query_bias_grad = jnp.sum(query_low_t.astype(jnp.float32), axis=1)
    value_bias_grad = jnp.sum(kv_low[:, local_width:].astype(jnp.float32), axis=0)
    unused_first, norm_one_pull = jax.vjp(layer_norm, inputs32, attn_norm_gain, attn_norm_bias)
    input_part, attn_norm_gain_grad, attn_norm_bias_grad = norm_one_pull(normed_one_grad)
    input_grad = (resid_grad + input_part).astype(jnp.bfloat16)
    vectors = [
        attn_norm_gain_grad,
        attn_norm_bias_grad,
        output_bias_grad,
        feed_norm_gain_grad,
        feed_norm_bias_grad,
        expand_bias_grad,
        shrink_bias_grad,
        query_bias_grad,
        value_bias_grad,
    ]
    joined = sum_tokens_small(jnp.concatenate(vectors))
    summed = []
    first = 0
    for vector in vectors:
        summed.append(joined[first : first + vector.shape[0]])
        first += vector.shape[0]
    ff_rows = shrink_weight.shape[0]
    return (
        block_output,
        input_grad,
        summed[0],
        summed[1],
        input_weight_grad,
        jnp.stack([summed[7], summed[8]]),
        output_weight_grad,
        summed[2],
        summed[3],
        summed[4],
        feed_grads[ff_rows:],
        summed[5],
        feed_grads[:ff_rows],
        summed[6],
    )


def solution(mesh):
    placed = (
        P("dp", None),
        P(),
        P(),
        P(),
        P(None, None, "tensor"),
        P(None, "tensor"),
        P("tensor", None),
        P(),
        P(),
        P(),
        P(None, "tensor"),
        P("tensor"),
        P("tensor", None),
        P(),
        P("dp", None),
    )
    return jax.shard_map(
        local,
        mesh=mesh,
        in_specs=placed,
        out_specs=(
            P("dp", None),
            P("dp", None),
            P(),
            P(),
            P(None, None, "tensor"),
            P(None, "tensor"),
            P("tensor", None),
            P(),
            P(),
            P(),
            P(None, "tensor"),
            P("tensor"),
            P("tensor", None),
            P(),
        ),
        check_vma=False,
    )
```

```python
import functools

import jax
import jax.numpy as jnp
from jax import lax
from jax.experimental import pallas as pl
from jax.experimental.pallas import tpu as pltpu
from jax.sharding import PartitionSpec as P

HEAD_DIM = 64
GROUP = 8


EPSILON = 1e-05
MASKED_SCORE = -1e30
RING = (0, 2, 4, 6, 7, 5, 3, 1)
TILE = 256
VMEM_BYTES = 48 * 1024 * 1024


def ring_shift(value, step):
    pairs = []
    for first in range(0, lax.axis_size("dp"), GROUP):
        for place in range(GROUP):
            pairs.append((first + RING[place], first + RING[(place + step) % GROUP]))
    return lax.ppermute(value, "dp", pairs)


def tdot(left, right, left_dim, right_dim):
    return lax.dot_general(
        left, right, (((left_dim,), (right_dim,)), ((), ())), preferred_element_type=jnp.float32
    )


def forward_kernel(heads, blocks, diagonal, *refs):
    flags, q_ref = refs[:2]
    kv_refs = refs[2 : 2 + 2 * blocks]
    carry_in = refs[2 + 2 * blocks : -3]
    max_ref, sum_ref, acc_ref = refs[-3:]
    tile = q_ref.shape[1]
    if diagonal:
        max_ref[...] = jnp.full(max_ref.shape, MASKED_SCORE, jnp.float32)
        sum_ref[...] = jnp.zeros(sum_ref.shape, jnp.float32)
        acc_ref[...] = jnp.zeros(acc_ref.shape, jnp.float32)
    else:
        max_ref[...] = carry_in[0][...]
        sum_ref[...] = carry_in[1][...]
        acc_ref[...] = carry_in[2][...]
    first_query = pl.program_id(0) * tile

    def block(k_ref, v_ref):
        spans = [slice(head * HEAD_DIM, (head + 1) * HEAD_DIM) for head in range(heads)]
        scores = [tdot(k_ref[rows, :], q_ref[rows, :], 0, 0) for rows in spans]
        if diagonal:
            key_place = lax.broadcasted_iota(jnp.int32, scores[0].shape, 0)
            query_place = lax.broadcasted_iota(jnp.int32, scores[0].shape, 1) + first_query
            allowed = key_place <= query_place
            scores = [jnp.where(allowed, part, MASKED_SCORE) for part in scores]
        olds = [max_ref[head : head + 1, :] for head in range(heads)]
        sums = [sum_ref[head : head + 1, :] for head in range(heads)]
        accs = [acc_ref[rows, :] for rows in spans]
        news = [
            jnp.maximum(old, jnp.max(part, axis=0, keepdims=True))
            for old, part in zip(olds, scores)
        ]
        weights = [jnp.exp(part - new) for part, new in zip(scores, news)]
        shrinks = [jnp.exp(old - new) for old, new in zip(olds, news)]
        sums = [
            total * shrink + jnp.sum(part, axis=0, keepdims=True)
            for total, shrink, part in zip(sums, shrinks, weights)
        ]
        accs = [
            acc * shrink + tdot(v_ref[rows, :], part.astype(jnp.bfloat16), 1, 0)
            for acc, shrink, rows, part in zip(accs, shrinks, spans, weights)
        ]
        for head, rows in enumerate(spans):
            max_ref[head : head + 1, :] = news[head]
            sum_ref[head : head + 1, :] = sums[head]
            acc_ref[rows, :] = accs[head]

    for index in range(blocks):
        k_ref, v_ref = kv_refs[2 * index : 2 * index + 2]
        if diagonal:
            block(k_ref, v_ref)
        else:
            pl.when(flags[index] > 0)(functools.partial(block, k_ref, v_ref))


def attend_forward(flags, query_t, blocks, carried):
    width, tokens = query_t.shape
    heads = width // HEAD_DIM
    diagonal = carried is None
    in_specs = [
        pl.BlockSpec(memory_space=pltpu.SMEM),
        pl.BlockSpec((width, TILE), lambda i: (0, i)),
    ]
    operands = [flags, query_t]
    for pair in blocks:
        for array, half in pair:
            in_specs.append(pl.BlockSpec((width, tokens), lambda i, half=half: (half, 0)))
            operands.append(array)
    carry_specs = [
        pl.BlockSpec((heads, TILE), lambda i: (0, i)),
        pl.BlockSpec((heads, TILE), lambda i: (0, i)),
        pl.BlockSpec((width, TILE), lambda i: (0, i)),
    ]
    if not diagonal:
        in_specs.extend(carry_specs)
        operands.extend(carried)
    pairs = len(blocks) * heads * tokens * tokens
    return pl.pallas_call(
        functools.partial(forward_kernel, heads, len(blocks), diagonal),
        grid=(tokens // TILE,),
        in_specs=in_specs,
        out_specs=carry_specs,
        out_shape=[
            jax.ShapeDtypeStruct((heads, tokens), jnp.float32),
            jax.ShapeDtypeStruct((heads, tokens), jnp.float32),
            jax.ShapeDtypeStruct((width, tokens), jnp.float32),
        ],
        compiler_params=pltpu.CompilerParams(vmem_limit_bytes=VMEM_BYTES),
        cost_estimate=pl.CostEstimate(
            flops=16 * pairs * HEAD_DIM, bytes_accessed=4 * width * tokens * 4, transcendentals=pairs
        ),
    )(*operands)


def backward_kernel(heads, blocks, diagonal, *refs):
    flags, q_ref, grad_ref, log_ref, delta_ref = refs[:5]
    kv_refs = refs[5 : 5 + 2 * blocks]
    query_in = refs[5 + 2 * blocks]
    query_out = refs[6 + 2 * blocks]
    kv_out = refs[7 + 2 * blocks :]
    step = pl.program_id(0)
    tile = kv_refs[0].shape[1]
    width = heads * HEAD_DIM

    @pl.when(step == 0)
    def start():
        query_out[...] = query_in[...]

    def block(k_ref, v_ref, out_ref):
        for head in range(heads):
            rows = slice(head * HEAD_DIM, (head + 1) * HEAD_DIM)
            query = q_ref[rows, :]
            grad = grad_ref[rows, :]
            key = k_ref[rows, :]
            scores = tdot(key, query, 0, 0)
            probs = jnp.exp(scores - log_ref[head : head + 1, :])
            if diagonal:
                key_place = lax.broadcasted_iota(jnp.int32, scores.shape, 0) + step * tile
                query_place = lax.broadcasted_iota(jnp.int32, scores.shape, 1)
                probs = jnp.where(key_place <= query_place, probs, 0.0)
            prob_grad = tdot(v_ref[rows, :], grad, 0, 0)
            score_grad = (probs * (prob_grad - delta_ref[head : head + 1, :])).astype(jnp.bfloat16)
            out_ref[:, rows] = tdot(score_grad, query, 1, 1)
            out_ref[:, width + head * HEAD_DIM : width + (head + 1) * HEAD_DIM] = tdot(
                probs.astype(jnp.bfloat16), grad, 1, 1
            )
            query_out[rows, :] += tdot(key, score_grad, 1, 0)

    for index in range(blocks):
        k_ref, v_ref = kv_refs[2 * index : 2 * index + 2]
        out_ref = kv_out[index]
        if diagonal:
            block(k_ref, v_ref, out_ref)
        else:
            pl.when(flags[index] > 0)(functools.partial(block, k_ref, v_ref, out_ref))

            @pl.when(flags[index] <= 0)
            def empty(out_ref=out_ref):
                out_ref[...] = jnp.zeros(out_ref.shape, jnp.float32)


def attend_backward(flags, query_t, grad_t, log_total, delta, blocks, query_sum, diagonal):
    width, tokens = query_t.shape
    heads = width // HEAD_DIM
    whole = lambda rows: pl.BlockSpec((rows, tokens), lambda i: (0, 0))
    in_specs = [
        pl.BlockSpec(memory_space=pltpu.SMEM),
        whole(width),
        whole(width),
        whole(heads),
        whole(heads),
    ]
    operands = [flags, query_t, grad_t, log_total, delta]
    for pair in blocks:
        for array, half in pair:
            in_specs.append(pl.BlockSpec((width, TILE), lambda i, half=half: (half, i)))
            operands.append(array)
    in_specs.append(whole(width))
    operands.append(query_sum)
    pairs = len(blocks) * heads * tokens * tokens
    return pl.pallas_call(
        functools.partial(backward_kernel, heads, len(blocks), diagonal),
        grid=(tokens // TILE,),
        in_specs=in_specs,
        out_specs=[whole(width)]
        + [pl.BlockSpec((TILE, 2 * width), lambda i: (i, 0)) for unused in blocks],
        out_shape=[jax.ShapeDtypeStruct((width, tokens), jnp.float32)]
        + [jax.ShapeDtypeStruct((tokens, 2 * width), jnp.float32) for unused in blocks],
        compiler_params=pltpu.CompilerParams(vmem_limit_bytes=VMEM_BYTES),
        cost_estimate=pl.CostEstimate(
            flops=40 * pairs * HEAD_DIM, bytes_accessed=6 * width * tokens * 4, transcendentals=pairs
        ),
    )(*operands)


def layer_norm(rows, gain, bias_vec):
    center = jnp.mean(rows, axis=-1, keepdims=True)
    centred = rows - center
    spread = jnp.mean(centred * centred, axis=-1, keepdims=True)
    return centred * lax.rsqrt(spread + EPSILON) * gain + bias_vec


def gelu_tanh(values):
    return jax.nn.gelu(values, approximate=True)


def partner(value, axis, mask):
    pairs = [(source, source ^ mask) for source in range(lax.axis_size(axis))]
    return lax.ppermute(value, axis, pairs)


def sum_tokens_small(value):
    mask = 1
    while mask < lax.axis_size("dp"):
        value = value + partner(value, "dp", mask)
        mask *= 2
    return value


def rounded(value):
    return lax.optimization_barrier(value.astype(jnp.bfloat16))


def scatter_pair(value):
    upper = lax.axis_index("dp") % 2
    half = value.shape[0] // 2
    kept = lax.dynamic_slice_in_dim(value, upper * half, half, 0)
    sent = lax.dynamic_slice_in_dim(value, (1 - upper) * half, half, 0)
    return rounded(kept.astype(jnp.float32) + partner(sent, "dp", 1).astype(jnp.float32))


def scatter_four(value):
    place = lax.axis_index("dp") // 2 % 4
    quarter = value.shape[0] // 4
    total = lax.dynamic_slice_in_dim(value, place * quarter, quarter, 0).astype(jnp.float32)
    for apart in (1, 2, 3):
        sent = lax.dynamic_slice_in_dim(value, (place ^ apart) * quarter, quarter, 0)
        total = total + partner(sent, "dp", 2 * apart).astype(jnp.float32)
    mask = GROUP
    while mask < lax.axis_size("dp"):
        low = rounded(total)
        total = low.astype(jnp.float32) + partner(low, "dp", mask).astype(jnp.float32)
        mask *= 2
    return rounded(total)


def gather_four(value):
    place = lax.axis_index("dp") // 2 % 4
    quarter = value.shape[0]
    joined = jnp.zeros((4 * quarter, value.shape[1]), value.dtype)
    joined = lax.dynamic_update_slice_in_dim(joined, value, place * quarter, 0)
    for apart in (1, 2, 3):
        other = partner(value, "dp", 2 * apart)
        joined = lax.dynamic_update_slice_in_dim(joined, other, (place ^ apart) * quarter, 0)
    return joined


def gather_pair(value):
    upper = lax.axis_index("dp") % 2
    other = partner(value, "dp", 1)
    return jnp.concatenate(
        [jnp.where(upper == 0, value, other), jnp.where(upper == 0, other, value)], axis=0
    )


def sum_tensor(value):
    value = rounded(value)
    core = lax.axis_index("tensor") % 2
    half = value.shape[0] // 2
    kept = lax.dynamic_slice_in_dim(value, core * half, half, 0)
    sent = lax.dynamic_slice_in_dim(value, (1 - core) * half, half, 0)
    total = kept.astype(jnp.float32) + partner(sent, "tensor", 1).astype(jnp.float32)
    mask = 2
    while mask < lax.axis_size("tensor"):
        low = rounded(total)
        total = low.astype(jnp.float32) + partner(low, "tensor", mask).astype(jnp.float32)
        mask *= 2
    low = rounded(total)
    other = partner(low, "tensor", 1)
    lower = jnp.where(core == 0, low, other)
    upper = jnp.where(core == 0, other, low)
    return jnp.concatenate([lower, upper], axis=0).astype(jnp.float32)


def local(
    block_input,
    block_order,
    attn_norm_gain,
    attn_norm_bias,
    input_weight,
    query_value_bias,
    output_weight,
    output_bias,
    feed_norm_gain,
    feed_norm_bias,
    expand_weight,
    expand_bias,
    shrink_weight,
    shrink_bias,
    output_grad,
):
    dp_index = lax.axis_index("dp")
    tok_rows = block_input.shape[0]
    local_width = input_weight.shape[2]
    local_heads = local_width // HEAD_DIM
    scale = HEAD_DIM ** (-0.5)
    order_row = lax.dynamic_index_in_dim(block_order, dp_index // GROUP, 0, keepdims=False)
    ring_order = order_row[jnp.array(RING)]
    ring_place = jnp.argmax(jnp.array(RING) == dp_index % GROUP).astype(jnp.int32)
    own_block = ring_order[ring_place]

    def flags_of(*offsets):
        return jnp.stack(
            [
                (ring_order[(ring_place + offset) % GROUP] < own_block).astype(jnp.int32)
                for offset in offsets
            ]
        )

    inputs32 = block_input.astype(jnp.float32)
    normed_one = layer_norm(inputs32, attn_norm_gain, attn_norm_bias).astype(jnp.bfloat16)
    kv_weight = jnp.concatenate([input_weight[1], input_weight[2]], axis=1)
    kv_bias = jnp.concatenate([jnp.zeros((local_width,), jnp.float32), query_value_bias[1]])
    kv_t = (
        jnp.einsum("td,df->ft", normed_one, kv_weight, preferred_element_type=jnp.float32)
        + kv_bias[:, None]
    ).astype(jnp.bfloat16)
    ups = [kv_t]
    downs = [kv_t]
    ups.append(ring_shift(ups[0], 1))
    downs.append(ring_shift(downs[0], -1))
    query_t = (
        jnp.einsum("td,df->ft", normed_one, input_weight[0], preferred_element_type=jnp.float32)
        + query_value_bias[0][:, None]
    ).astype(jnp.bfloat16)
    query_t = query_t * jnp.bfloat16(scale)
    def whole_pair(array):
        return ((array, 0), (array, 1))

    own_pair = [whole_pair(kv_t)]
    hop_pairs = [None]
    hop_flags = [None] + [flags_of(-hop, hop) for hop in (1, 2, 3)]
    far_flags = flags_of(4)
    carried = attend_forward(far_flags, query_t, own_pair, None)
    for hop in (1, 2, 3):
        ups[hop], downs[hop], carried = lax.optimization_barrier((ups[hop], downs[hop], carried))
        hop_pairs.append([whole_pair(ups[hop]), whole_pair(downs[hop])])
        if hop < 3:
            ups.append(ring_shift(ups[hop], 1))
            downs.append(ring_shift(downs[hop], -1))
        else:
            far_keys = ring_shift(ups[hop][:local_width], 1)
            far_values = ring_shift(downs[hop][local_width:], -1)
            far_pair = [((far_keys, 0), (far_values, 0))]
        carried = attend_forward(hop_flags[hop], query_t, hop_pairs[hop], carried)
    run_max, run_sum, acc = attend_forward(far_flags, query_t, far_pair, carried)
    log_total = run_max + jnp.log(run_sum)
    context_t = (acc.reshape(local_heads, HEAD_DIM, tok_rows) / run_sum[:, None, :]).reshape(
        local_width, tok_rows
    )
    context_low_t = context_t.astype(jnp.bfloat16)
    attn_part = jnp.einsum(
        "ct,cd->td", context_low_t, output_weight, preferred_element_type=jnp.float32
    )
    resid = inputs32 + sum_tensor(attn_part) + output_bias
    normed_two = layer_norm(resid, feed_norm_gain, feed_norm_bias).astype(jnp.bfloat16)
    hidden_pre = (
        jnp.dot(normed_two, expand_weight, preferred_element_type=jnp.float32) + expand_bias
    )
    hidden_grad = jnp.einsum(
        "td,fd->tf", output_grad, shrink_weight, preferred_element_type=jnp.float32
    )
    hidden, gelu_pull = jax.vjp(gelu_tanh, hidden_pre)
    hidden_low = hidden.astype(jnp.bfloat16)
    pre_grad = gelu_pull(hidden_grad)[0].astype(jnp.bfloat16)
    two_part = jnp.einsum("tf,df->td", pre_grad, expand_weight, preferred_element_type=jnp.float32)
    normed_two_grad = sum_tensor(two_part)
    feed_part = jnp.dot(
        hidden_low, shrink_weight, preferred_element_type=jnp.float32
    ).astype(jnp.bfloat16)
    grad_out32 = output_grad.astype(jnp.float32)
    shrink_weight_grad = jnp.einsum(
        "tf,td->fd", hidden_low, output_grad, preferred_element_type=jnp.float32
    )
    expand_weight_grad = jnp.einsum(
        "td,tf->df", normed_two, pre_grad, preferred_element_type=jnp.float32
    )
    feed_low = scatter_pair(
        jnp.concatenate([shrink_weight_grad, expand_weight_grad], axis=0).astype(jnp.bfloat16)
    )
    shrink_bias_grad = jnp.sum(grad_out32, axis=0)
    expand_bias_grad = jnp.sum(pre_grad.astype(jnp.float32), axis=0)
    unused_norm, norm_two_pull = jax.vjp(layer_norm, resid, feed_norm_gain, feed_norm_bias)
    resid_part, feed_norm_gain_grad, feed_norm_bias_grad = norm_two_pull(normed_two_grad)
    resid_grad = grad_out32 + resid_part
    branch_grad = resid_grad.astype(jnp.bfloat16)
    output_bias_grad = jnp.sum(branch_grad.astype(jnp.float32), axis=0)
    grad_t = jnp.einsum(
        "td,cd->ct", branch_grad, output_weight, preferred_element_type=jnp.float32
    ).astype(jnp.bfloat16)
    delta = jnp.sum(
        (grad_t.astype(jnp.float32) * context_t).reshape(local_heads, HEAD_DIM, tok_rows), axis=1
    )

    delta, feed_low = lax.optimization_barrier((delta, feed_low))

    def back(flags, blocks, query_sum, diagonal):
        return attend_backward(
            flags, query_t, grad_t, log_total, delta, blocks, query_sum, diagonal
        )

    query_sum = jnp.zeros((local_width, tok_rows), jnp.float32)
    query_sum, far_term = back(far_flags, far_pair, query_sum, False)
    query_sum, feed_part = lax.optimization_barrier((query_sum, feed_part))
    block_output = (resid + sum_tensor(feed_part) + shrink_bias).astype(jnp.bfloat16)
    far_low = far_term.astype(jnp.bfloat16)
    moving_up = ring_shift(far_low[:, :local_width], 1)
    moving_down = ring_shift(far_low[:, local_width:], -1)
    for hop in (3, 2, 1):
        if hop == 2:
            query_sum, feed_low = lax.optimization_barrier((query_sum, feed_low))
            feed_low = scatter_four(feed_low)
        if hop == 1:
            query_sum, feed_low, block_output = lax.optimization_barrier(
                (query_sum, feed_low, block_output)
            )
            feed_low = gather_four(feed_low)
        query_sum, down_term, up_term = back(hop_flags[hop], hop_pairs[hop], query_sum, False)
        if hop == 3:
            up_sum = jnp.concatenate(
                [
                    up_term[:, :local_width] + moving_up.astype(jnp.float32),
                    up_term[:, local_width:],
                ],
                axis=1,
            )
            down_sum = jnp.concatenate(
                [
                    down_term[:, :local_width],
                    down_term[:, local_width:] + moving_down.astype(jnp.float32),
                ],
                axis=1,
            )
        else:
            up_sum = up_term + moving_up.astype(jnp.float32)
            down_sum = down_term + moving_down.astype(jnp.float32)
        up_low, down_low, query_sum = lax.optimization_barrier(
            (up_sum.astype(jnp.bfloat16), down_sum.astype(jnp.bfloat16), query_sum)
        )
        moving_up = ring_shift(up_low, 1)
        moving_down = ring_shift(down_low, -1)
    query_sum, own_term = back(far_flags, own_pair, query_sum, True)
    kv_low = (
        own_term + moving_up.astype(jnp.float32) + moving_down.astype(jnp.float32)
    ).astype(jnp.bfloat16)
    query_low_t = (query_sum * scale).astype(jnp.bfloat16)
    output_weight_grad_t = jnp.einsum(
        "ct,td->dc", context_low_t, branch_grad, preferred_element_type=jnp.float32
    )
    query_weight_grad = jnp.einsum(
        "td,ft->df", normed_one, query_low_t, preferred_element_type=jnp.float32
    )
    kv_weight_grad = jnp.einsum(
        "td,tf->df", normed_one, kv_low, preferred_element_type=jnp.float32
    )
    attn_low = jnp.concatenate(
        [query_weight_grad, kv_weight_grad, output_weight_grad_t], axis=1
    ).astype(jnp.bfloat16)
    attn_low, feed_low, kv_low = lax.optimization_barrier((attn_low, feed_low, kv_low))
    attn_low, feed_low = lax.optimization_barrier((scatter_pair(attn_low), feed_low))
    feed_low = gather_pair(feed_low)
    attn_low, feed_low = lax.optimization_barrier((gather_four(scatter_four(attn_low)), feed_low))
    feed_grads = feed_low.astype(jnp.float32)
    attn_grads = gather_pair(attn_low).astype(jnp.float32)
    one_part = jnp.einsum(
        "ft,df->td", query_low_t, input_weight[0], preferred_element_type=jnp.float32
    ) + jnp.einsum("tf,df->td", kv_low, kv_weight, preferred_element_type=jnp.float32)
    normed_one_grad = sum_tensor(one_part)
    input_weight_grad = jnp.stack(
        [attn_grads[:, j * local_width : (j + 1) * local_width] for j in range(3)]
    )
    output_weight_grad = jnp.transpose(attn_grads[:, 3 * local_width :])
    query_bias_grad = jnp.sum(query_low_t.astype(jnp.float32), axis=1)
    value_bias_grad = jnp.sum(kv_low[:, local_width:].astype(jnp.float32), axis=0)
    unused_first, norm_one_pull = jax.vjp(layer_norm, inputs32, attn_norm_gain, attn_norm_bias)
    input_part, attn_norm_gain_grad, attn_norm_bias_grad = norm_one_pull(normed_one_grad)
    input_grad = (resid_grad + input_part).astype(jnp.bfloat16)
    vectors = [
        attn_norm_gain_grad,
        attn_norm_bias_grad,
        output_bias_grad,
        feed_norm_gain_grad,
        feed_norm_bias_grad,
        expand_bias_grad,
        shrink_bias_grad,
        query_bias_grad,
        value_bias_grad,
    ]
    joined = sum_tokens_small(jnp.concatenate(vectors))
    summed = []
    first = 0
    for vector in vectors:
        summed.append(joined[first : first + vector.shape[0]])
        first += vector.shape[0]
    ff_rows = shrink_weight.shape[0]
    return (
        block_output,
        input_grad,
        summed[0],
        summed[1],
        input_weight_grad,
        jnp.stack([summed[7], summed[8]]),
        output_weight_grad,
        summed[2],
        summed[3],
        summed[4],
        feed_grads[ff_rows:],
        summed[5],
        feed_grads[:ff_rows],
        summed[6],
    )


def solution(mesh):
    placed = (
        P("dp", None),
        P(),
        P(),
        P(),
        P(None, None, "tensor"),
        P(None, "tensor"),
        P("tensor", None),
        P(),
        P(),
        P(),
        P(None, "tensor"),
        P("tensor"),
        P("tensor", None),
        P(),
        P("dp", None),
    )
    return jax.shard_map(
        local,
        mesh=mesh,
        in_specs=placed,
        out_specs=(
            P("dp", None),
            P("dp", None),
            P(),
            P(),
            P(None, None, "tensor"),
            P(None, "tensor"),
            P("tensor", None),
            P(),
            P(),
            P(),
            P(None, "tensor"),
            P("tensor"),
            P("tensor", None),
            P(),
        ),
        check_vma=False,
    )
```
